1024 devices in a mesh: loop: 32 (over z_hi, x, core), group: 32 (over z_lo, y).
Axes of the slice: x: 4, y: 4, z: 32 (z_hi: 4, z_lo: 8; z = z_hi * 8 + z_lo), core: 2. Of those that a mesh axis runs over, the one named last changes fastest.
Arguments:
- images: bfloat16 [8192, 1152], P(('loop', 'group')), may hold values from -0.1875 to 0.1875
- texts: bfloat16 [8192, 1152], P(('loop', 'group')), may hold values from -0.1875 to 0.1875
- scale: float32 [], replicated, may hold values from 4 to 10
- bias: float32 [], replicated, may hold values from -3 to -1
Outputs:
- image_grad: float32 [8192, 1152], P(('loop', 'group'))
- text_grad: float32 [8192, 1152], P(('loop', 'group'))
- image_loss: float32 [8192], P(('loop', 'group'))
The draws below stay inside these ranges and needn't reach their ends.
All inputs are finite; a program needn't handle non-finite values.
Results may differ from the reference program's by a relative error of at most 0.0044.
Values may be sent and summed in bfloat16 or wider, within the bound.
No kernel may reach another device: no remote copies, remote signals or barrier semaphores. Data moves between devices by JAX's collectives and lax.ppermute only.
A program may use at most 32 MiB of HBM per device.

```python
import math
import jax
import jax.numpy as jnp
from jax import lax

D = 1152
ROWS = 8
ROUNDS = 3
PAIRS = 8192
N_LOOP = 32
N_GROUP = 32


def shard_levels(own_key, extent, split, least, largest):
    loudness = 1.0
    for dim, shards_of in split:
        draws = jax.random.uniform(jax.random.fold_in(jax.random.fold_in(own_key, 6), dim), (shards_of,), jnp.float32, least / len(split), largest / len(split))
        loudness = loudness * jnp.repeat(jnp.exp(draws), extent[dim] // shards_of).reshape((-1,) + (1,) * (len(extent) - 1 - dim))
    return loudness


def centred(rng, shape, spread, most, cuts=(), kind=jnp.bfloat16):
    entries = spread * jax.random.normal(rng, shape, jnp.float32)
    if cuts:
        entries = entries * shard_levels(rng, shape, cuts, -0.22, 0.18)
    return jnp.clip(entries, -most, most).astype(kind)


def setup_inputs(seed: int = 0) -> dict:
    streams_of = jax.random.split(jax.random.key(seed), 5)
    return {
        "images": centred(streams_of[0], (PAIRS, D), D ** -0.5, 0.1875, ((0, 1024),)),
        "texts": centred(streams_of[1], (PAIRS, D), D ** -0.5, 0.1875, ((0, 1024),)),
        "scale": jnp.clip(jnp.exp(jax.random.uniform(streams_of[2], (), jnp.float32, math.log(4.0), math.log(10.0))), 4.0, 10.0),
        "bias": jnp.clip(jax.random.uniform(streams_of[3], (), jnp.float32, -3.0, -1.0), -3.0, -1.0),
    }


EPS = 1e-06

def normalize(x):
    xf = x.astype(jnp.float32)
    norms = jnp.sqrt(lax.optimization_barrier(jnp.sum(xf * xf, axis=-1, keepdims=True)) + EPS)
    return (xf / norms, norms)

def project_back(grad, unit, norms):
    return (grad - unit * lax.optimization_barrier(jnp.sum(unit * grad, axis=-1, keepdims=True))) / norms

def reference(images, texts, scale, bias):
    unit_img, norm_img = normalize(images)
    unit_txt, norm_txt = normalize(texts)
    img_blocks = unit_img.astype(jnp.bfloat16).reshape(N_LOOP, N_GROUP, ROWS, D)
    txt_blocks = unit_txt.astype(jnp.bfloat16).reshape(N_LOOP, N_GROUP * ROWS, D)
    temper = scale.astype(jnp.float32)
    offset = bias.astype(jnp.float32)
    width = N_GROUP * ROWS
    column = jnp.arange(width, dtype=jnp.int32)[None, None, :]
    target = jnp.arange(N_GROUP, dtype=jnp.int32)[:, None, None] * ROWS + jnp.arange(ROWS, dtype=jnp.int32)[None, :, None]
    positive = jnp.where(column == target, 1.0, -1.0).astype(jnp.float32)

    def one_block(position):
        imgs = img_blocks[position].astype(jnp.float32)
        losses = jnp.zeros((N_GROUP, ROWS), jnp.float32)
        grads = jnp.zeros((N_GROUP, ROWS, D), jnp.float32)
        pieces = []
        for step in range(ROUNDS):
            source = (position - step) % N_LOOP
            block = lax.dynamic_index_in_dim(txt_blocks, source, 0, keepdims=False).astype(jnp.float32)
            logit = temper * jnp.einsum('gid,jd->gij', imgs, block) + offset
            if step == 0:
                sign = positive
            else:
                sign = -jnp.ones_like(logit)
            losses = losses + lax.optimization_barrier(jnp.sum(jax.nn.softplus(-sign * logit), axis=-1))
            coef = (-sign * jax.nn.sigmoid(-sign * logit) * temper).astype(jnp.bfloat16).astype(jnp.float32)
            grads = grads + jnp.einsum('gij,jd->gid', coef, block)
            pieces.append(jnp.einsum('gij,gid->jd', coef, imgs))
        return (losses, grads, jnp.stack(pieces))
    losses, grads, pieces = lax.map(one_block, jnp.arange(N_LOOP, dtype=jnp.int32))
    text_total = jnp.zeros((N_LOOP, width, D), jnp.float32)
    for step in range(ROUNDS):
        text_total = text_total + jnp.roll(pieces[:, step], -step, axis=0)
    image_grad = project_back(grads.reshape(PAIRS, D), unit_img, norm_img)
    text_grad = project_back(text_total.reshape(PAIRS, D), unit_txt, norm_txt)
    return (image_grad, text_grad, losses.reshape(PAIRS))
```

```python
import jax
import jax.numpy as jnp
from jax import lax
from jax.experimental import pallas as pl
from jax.experimental.pallas import tpu as pltpu
from jax.sharding import Mesh, PartitionSpec as P

EPS = 1e-06
ROUNDS = 3
ROWS = 8
FAR, X, CORE, LINE, RING = 4, 4, 2, 8, 4
LOOP = ("far", "x", "core")
LANES = 128


def passed_along(value, steps):
    count = FAR * X * CORE
    return lax.ppermute(value, LOOP, [(s, (s + steps) % count) for s in range(count)])


def normalize(x):
    xf = x.astype(jnp.float32)
    norms = jnp.sqrt(jnp.sum(xf * xf, axis=-1, keepdims=True) + EPS)
    return xf / norms, norms


def project_back(grad, unit, norms):
    return (grad - unit * jnp.sum(unit * grad, axis=-1, keepdims=True)) / norms


def score_kernel(place_ref, param_ref, img_ref, txt_ref, gu_ref, gv_ref):
    scale, bias = param_ref[0], param_ref[1]
    img = normalize(img_ref[...])[0].astype(jnp.bfloat16)
    txt = normalize(txt_ref[...])[0].astype(jnp.bfloat16)
    dots = lax.dot_general(img, txt, (((1,), (1,)), ((), ())), preferred_element_type=jnp.float32)
    logit = scale * dots + bias
    row = lax.broadcasted_iota(jnp.int32, logit.shape, 0) - place_ref[0] * ROWS
    column = lax.broadcasted_iota(jnp.int32, logit.shape, 1) - place_ref[1] * (ROUNDS * ROWS)
    own = (row == column) & (row >= 0) & (row < ROWS)
    against = jnp.where(own, -logit, logit)
    decay = jnp.exp(-jnp.abs(against))
    loss = jnp.maximum(against, 0.0) + jnp.log1p(decay)
    chance = jnp.where(against >= 0, 1.0, decay) / (1.0 + decay)
    coef = jnp.where(own, -chance, chance) * scale
    width = img.shape[1]
    gu_ref[:, :width] = jnp.dot(
        coef.astype(jnp.bfloat16), txt, preferred_element_type=jnp.float32
    ).astype(jnp.bfloat16)
    gv_ref[...] = jnp.dot(
        coef.T.astype(jnp.bfloat16), img, preferred_element_type=jnp.float32
    ).astype(jnp.bfloat16)
    total = jnp.sum(loss, axis=1, keepdims=True)
    high = total.astype(jnp.bfloat16).astype(jnp.float32)
    lane = lax.broadcasted_iota(jnp.int32, (total.shape[0], LANES), 1)
    gu_ref[:, width:] = jnp.where(
        lane == 0, high, jnp.where(lane == 1, total - high, 0.0)
    ).astype(jnp.bfloat16)


def ring_sum_kernel(parts_ref, own_ref, back1_ref, back2_ref):
    parts = parts_ref[...].astype(jnp.float32)
    total = jnp.sum(parts.reshape(RING, ROUNDS * ROWS, parts.shape[1]), axis=0)
    own_ref[...] = total[:ROWS]
    back1_ref[...] = total[ROWS : 2 * ROWS]
    back2_ref[...] = total[2 * ROWS :]


def finish_kernel(parts_ref, img_ref, txt_ref, own_ref, back1_ref, back2_ref, ig_ref, tg_ref, loss_ref):
    width = img_ref.shape[1]
    parts = parts_ref[...].astype(jnp.float32)
    total = jnp.sum(parts.reshape(LINE, ROWS, parts.shape[1]), axis=0)
    ig_ref[...] = project_back(total[:, :width], *normalize(img_ref[...]))
    gv = own_ref[...] + back1_ref[...] + back2_ref[...]
    tg_ref[...] = project_back(gv, *normalize(txt_ref[...]))
    loss = jnp.sum(total[:, width:], axis=1, keepdims=True)
    row = lax.broadcasted_iota(jnp.int32, (ROWS, LANES), 0)
    lane = lax.broadcasted_iota(jnp.int32, (ROWS, LANES), 1)
    loss_ref[...] = jnp.sum(jnp.where(row == lane, loss, 0.0), axis=0, keepdims=True)


def on_device(images, texts, scale, bias):
    width = images.shape[1]
    place = jnp.stack([lax.axis_index("line"), lax.axis_index("ring")]).astype(jnp.int32)
    params = jnp.stack([scale, bias])
    before1 = passed_along(texts, 1)
    before2 = passed_along(texts, 2)
    line_imgs = lax.all_to_all(
        jnp.broadcast_to(images[None], (LINE, ROWS, width)), "line", 0, 0, tiled=True
    ).reshape(LINE * ROWS, width)
    visiting = jnp.concatenate([texts, before1, before2])
    visiting, line_imgs = lax.optimization_barrier((visiting, line_imgs))
    ring_txts = lax.all_to_all(
        jnp.broadcast_to(visiting[None], (RING, ROUNDS * ROWS, width)), "ring", 0, 0, tiled=True
    ).reshape(RING * ROUNDS * ROWS, width)
    smem = pl.BlockSpec(memory_space=pltpu.SMEM)
    vmem = pl.BlockSpec(memory_space=pltpu.VMEM)
    gu_parts, gv_parts = pl.pallas_call(
        score_kernel,
        out_shape=(
            jax.ShapeDtypeStruct((LINE * ROWS, width + LANES), jnp.bfloat16),
            jax.ShapeDtypeStruct((RING * ROUNDS * ROWS, width), jnp.bfloat16),
        ),
        in_specs=[smem, smem, vmem, vmem],
        out_specs=(vmem, vmem),
        name="score",
    )(place, params, line_imgs, ring_txts)
    gv_parts = lax.all_to_all(
        gv_parts.reshape(RING, ROUNDS * ROWS, width), "ring", 0, 0, tiled=True
    ).reshape(RING * ROUNDS * ROWS, width)
    piece = jax.ShapeDtypeStruct((ROWS, width), jnp.float32)
    own, back1, back2 = pl.pallas_call(
        ring_sum_kernel, out_shape=(piece,) * 3, in_specs=[vmem], out_specs=(vmem,) * 3, name="ring_sum"
    )(gv_parts)
    gu_parts, own = lax.optimization_barrier((gu_parts, own))
    back1 = passed_along(back1, -1)
    back2 = passed_along(back2, -2)
    gu_parts = lax.all_to_all(
        gu_parts.reshape(LINE, ROWS, width + LANES), "line", 0, 0, tiled=True
    ).reshape(LINE * ROWS, width + LANES)
    image_grad, text_grad, loss = pl.pallas_call(
        finish_kernel,
        out_shape=(piece, piece, jax.ShapeDtypeStruct((1, LANES), jnp.float32)),
        in_specs=[vmem] * 6,
        out_specs=(vmem,) * 3,
        name="finish",
    )(gu_parts, images, texts, own, back1, back2)
    return image_grad, text_grad, loss[0, :ROWS]


def solution(mesh):
    parts = Mesh(
        mesh.devices.reshape(FAR, X, CORE, LINE, RING), ("far", "x", "core", "line", "ring")
    )
    rows = P(("far", "x", "core", "line", "ring"), None)
    return jax.shard_map(
        on_device,
        mesh=parts,
        in_specs=(rows, rows, P(), P()),
        out_specs=(rows, rows, P(("far", "x", "core", "line", "ring"))),
        check_vma=False,
    )
```

```python
import jax
import jax.numpy as jnp
from jax import lax
from jax.experimental import pallas as pl
from jax.experimental.pallas import tpu as pltpu
from jax.sharding import Mesh, PartitionSpec as P

EPS = 1e-06
ROUNDS = 3
ROWS = 8
AXES = ("far", "x", "core", "line", "ring")
FAR, X, CORE, LINE, RING = 4, 4, 2, 8, 4
CHIPS = ("far", "x")
NEAR = CORE * RING
LANES = 128
SMEM = pl.BlockSpec(memory_space=pltpu.SMEM)
VMEM = pl.BlockSpec(memory_space=pltpu.VMEM)


def next_chip(value, steps):
    count = FAR * X
    return lax.ppermute(value, CHIPS, [(s, (s + steps) % count) for s in range(count)])


def normalize(x):
    xf = x.astype(jnp.float32)
    norms = jnp.sqrt(jnp.sum(xf * xf, axis=-1, keepdims=True) + EPS)
    return xf / norms, norms


def project_back(grad, unit, norms):
    return (grad - unit * jnp.sum(unit * grad, axis=-1, keepdims=True)) / norms


def spread_kernel(img_ref, out_ref):
    img = img_ref[...].astype(jnp.float32)
    out_ref[...] = jnp.concatenate([img] * LINE).astype(out_ref.dtype)


def pair_kernel(own_ref, before_ref, out_ref):
    pair = [own_ref[...].astype(jnp.float32), before_ref[...].astype(jnp.float32)]
    out_ref[...] = jnp.concatenate(pair * NEAR).astype(out_ref.dtype)


def score_kernel(scale_ref, bias_ref, img_ref, txt_ref, gu_ref, gv_ref):
    scale, bias = scale_ref[0], bias_ref[0]
    core, line, ring = lax.axis_index("core"), lax.axis_index("line"), lax.axis_index("ring")
    img = normalize(img_ref[...])[0].astype(jnp.bfloat16)
    txt = normalize(txt_ref[...])[0].astype(jnp.bfloat16)
    dots = lax.dot_general(img, txt, (((1,), (1,)), ((), ())), preferred_element_type=jnp.float32)
    logit = scale * dots + bias
    row = lax.broadcasted_iota(jnp.int32, logit.shape, 0)
    column = lax.broadcasted_iota(jnp.int32, logit.shape, 1)
    back = core - column // (RING * 2 * ROWS) + 2 * (column // ROWS % 2)
    scored = (back >= 0) & (back < ROUNDS)
    row = row - line * ROWS
    own = (row >= 0) & (row < ROWS) & (column == (core * RING + ring) * (2 * ROWS) + row)
    against = jnp.where(own, -logit, logit)
    decay = jnp.exp(-jnp.abs(against))
    loss = jnp.where(scored, jnp.maximum(against, 0.0) + jnp.log1p(decay), 0.0)
    chance = jnp.where(against >= 0, 1.0, decay) / (1.0 + decay)
    coef = jnp.where(scored, jnp.where(own, -chance, chance) * scale, 0.0)
    width = img.shape[1]
    gv_ref[...] = jnp.dot(
        coef.T.astype(jnp.bfloat16), img, preferred_element_type=jnp.float32
    ).astype(jnp.bfloat16)
    gu_ref[:, :width] = jnp.dot(
        coef.astype(jnp.bfloat16), txt, preferred_element_type=jnp.float32
    ).astype(jnp.bfloat16)
    total = jnp.sum(loss, axis=1, keepdims=True)
    high = total.astype(jnp.bfloat16).astype(jnp.float32)
    lane = lax.broadcasted_iota(jnp.int32, (total.shape[0], LANES), 1)
    gu_ref[:, width:] = jnp.where(
        lane == 0, high, jnp.where(lane == 1, total - high, 0.0)
    ).astype(jnp.bfloat16)


def near_sum_kernel(parts_ref, own_ref, back_ref):
    parts = parts_ref[...].astype(jnp.float32)
    total = jnp.sum(parts.reshape(NEAR, 2 * ROWS, parts.shape[1]), axis=0)
    own_ref[...] = total[:ROWS]
    back_ref[...] = total[ROWS:].astype(back_ref.dtype)


def finish_kernel(parts_ref, img_ref, txt_ref, own_ref, back_ref, ig_ref, tg_ref, loss_ref):
    width = img_ref.shape[1]
    parts = parts_ref[...].astype(jnp.float32)
    total = jnp.sum(parts.reshape(LINE, ROWS, parts.shape[1]), axis=0)
    ig_ref[...] = project_back(total[:, :width], *normalize(img_ref[...]))
    gv = own_ref[...] + back_ref[...].astype(jnp.float32)
    tg_ref[...] = project_back(gv, *normalize(txt_ref[...]))
    loss = jnp.sum(total[:, width:], axis=1, keepdims=True)
    row = lax.broadcasted_iota(jnp.int32, (ROWS, ROWS), 0)
    lane = lax.broadcasted_iota(jnp.int32, (ROWS, ROWS), 1)
    loss_ref[...] = jnp.sum(jnp.where(row == lane, loss, 0.0), axis=0)


def on_device(images, texts, scale, bias):
    width = images.shape[1]
    half, full = jnp.bfloat16, jnp.float32

    def shape(rows, columns, kind):
        return jax.ShapeDtypeStruct((rows, columns), kind)

    def exchange(value, axes, peers):
        pieces = value.reshape(peers, value.shape[0] // peers, value.shape[1])
        return lax.all_to_all(pieces, axes, 0, 0, tiled=True).reshape(value.shape)

    before = next_chip(texts, 1)
    spread = pl.pallas_call(
        spread_kernel,
        out_shape=shape(LINE * ROWS, width, half),
        in_specs=[VMEM],
        out_specs=VMEM,
        cost_estimate=pl.CostEstimate(flops=10**10, bytes_accessed=10**6, transcendentals=0),
        name="spread",
    )(images)
    line_imgs = exchange(spread, "line", LINE)
    pairs = pl.pallas_call(
        pair_kernel,
        out_shape=shape(NEAR * 2 * ROWS, width, half),
        in_specs=[VMEM, VMEM],
        out_specs=VMEM,
        name="pair",
    )(texts, before)
    near_txts = exchange(pairs, ("core", "ring"), NEAR)
    gu_parts, gv_parts = pl.pallas_call(
        score_kernel,
        out_shape=(shape(LINE * ROWS, width + LANES, half), shape(NEAR * 2 * ROWS, width, half)),
        in_specs=[SMEM, SMEM, VMEM, VMEM],
        out_specs=(VMEM, VMEM),
        name="score",
    )(scale.reshape(1), bias.reshape(1), line_imgs, near_txts)
    gv_parts = exchange(gv_parts, ("core", "ring"), NEAR)
    gu_parts = exchange(gu_parts, "line", LINE)
    own, back = pl.pallas_call(
        near_sum_kernel,
        out_shape=(shape(ROWS, width, full), shape(ROWS, width, half)),
        in_specs=[VMEM],
        out_specs=(VMEM, VMEM),
        name="near_sum",
    )(gv_parts)
    back = next_chip(back, -1)
    return pl.pallas_call(
        finish_kernel,
        out_shape=(
            shape(ROWS, width, full),
            shape(ROWS, width, full),
            jax.ShapeDtypeStruct((ROWS,), full),
        ),
        in_specs=[VMEM] * 5,
        out_specs=(VMEM, VMEM, VMEM),
        name="finish",
    )(gu_parts, images, texts, own, back)


def solution(mesh):
    parts = Mesh(mesh.devices.reshape(FAR, X, CORE, LINE, RING), AXES)
    rows = P(AXES, None)
    return jax.shard_map(
        on_device,
        mesh=parts,
        in_specs=(rows, rows, P(), P()),
        out_specs=(rows, rows, P(AXES)),
        check_vma=False,
    )
```

```python
import jax
import jax.numpy as jnp
from jax import lax
from jax.experimental import pallas as pl
from jax.experimental.pallas import tpu as pltpu
from jax.sharding import Mesh, PartitionSpec as P

EPS = 1e-06
ROUNDS = 3
ROWS = 8
AXES = ("far", "x", "core", "line", "ring")
FAR, X, CORE, LINE, RING = 4, 4, 2, 8, 4
CHIPS = ("far", "x")
NEAR = CORE * RING
LANES = 128
SMEM = pl.BlockSpec(memory_space=pltpu.SMEM)
VMEM = pl.BlockSpec(memory_space=pltpu.VMEM)
ROOM = pltpu.CompilerParams(vmem_limit_bytes=8 * 2**20)


def next_chip(value, steps):
    count = FAR * X
    return lax.ppermute(value, CHIPS, [(s, (s + steps) % count) for s in range(count)])


def normalize(x):
    xf = x.astype(jnp.float32)
    norms = jnp.sqrt(jnp.sum(xf * xf, axis=-1, keepdims=True) + EPS)
    return xf / norms, norms


def project_back(grad, unit, norms):
    return (grad - unit * jnp.sum(unit * grad, axis=-1, keepdims=True)) / norms


def spread_kernel(img_ref, out_ref):
    img = img_ref[...].astype(jnp.float32)
    out_ref[...] = jnp.concatenate([img] * LINE).astype(out_ref.dtype)


def pair_kernel(own_ref, before_ref, out_ref):
    pair = [own_ref[...].astype(jnp.float32), before_ref[...].astype(jnp.float32)]
    out_ref[...] = jnp.concatenate(pair * NEAR).astype(out_ref.dtype)


def score_kernel(scale_ref, bias_ref, img_ref, txt_ref, gu_ref, gv_ref):
    scale, bias = scale_ref[0], bias_ref[0]
    core, line, ring = lax.axis_index("core"), lax.axis_index("line"), lax.axis_index("ring")
    img = normalize(img_ref[...])[0].astype(jnp.bfloat16)
    txt = normalize(txt_ref[...])[0].astype(jnp.bfloat16)
    dots = lax.dot_general(img, txt, (((1,), (1,)), ((), ())), preferred_element_type=jnp.float32)
    logit = scale * dots + bias
    row = lax.broadcasted_iota(jnp.int32, logit.shape, 0)
    column = lax.broadcasted_iota(jnp.int32, logit.shape, 1)
    back = core - column // (RING * 2 * ROWS) + 2 * (column // ROWS % 2)
    scored = (back >= 0) & (back < ROUNDS)
    row = row - line * ROWS
    own = (row >= 0) & (row < ROWS) & (column == (core * RING + ring) * (2 * ROWS) + row)
    against = jnp.where(own, -logit, logit)
    decay = jnp.exp(-jnp.abs(against))
    loss = jnp.where(scored, jnp.maximum(against, 0.0) + jnp.log1p(decay), 0.0)
    chance = jnp.where(against >= 0, 1.0, decay) / (1.0 + decay)
    coef = jnp.where(scored, jnp.where(own, -chance, chance) * scale, 0.0)
    width = img.shape[1]
    gv_ref[...] = jnp.dot(
        coef.T.astype(jnp.bfloat16), img, preferred_element_type=jnp.float32
    ).astype(jnp.bfloat16)
    gu_ref[:, :width] = jnp.dot(
        coef.astype(jnp.bfloat16), txt, preferred_element_type=jnp.float32
    ).astype(jnp.bfloat16)
    total = jnp.sum(loss, axis=1, keepdims=True)
    high = total.astype(jnp.bfloat16).astype(jnp.float32)
    lane = lax.broadcasted_iota(jnp.int32, (total.shape[0], LANES), 1)
    gu_ref[:, width:] = jnp.where(
        lane == 0, high, jnp.where(lane == 1, total - high, 0.0)
    ).astype(jnp.bfloat16)


def near_sum_kernel(parts_ref, own_ref, back_ref):
    parts = parts_ref[...].astype(jnp.float32)
    total = jnp.sum(parts.reshape(NEAR, 2 * ROWS, parts.shape[1]), axis=0)
    own_ref[...] = total[:ROWS]
    back_ref[...] = total[ROWS:].astype(back_ref.dtype)


def finish_kernel(parts_ref, img_ref, txt_ref, own_ref, back_ref, ig_ref, tg_ref, loss_ref):
    width = img_ref.shape[1]
    parts = parts_ref[...].astype(jnp.float32)
    total = jnp.sum(parts.reshape(LINE, ROWS, parts.shape[1]), axis=0)
    ig_ref[...] = project_back(total[:, :width], *normalize(img_ref[...]))
    gv = own_ref[...] + back_ref[...].astype(jnp.float32)
    tg_ref[...] = project_back(gv, *normalize(txt_ref[...]))
    loss = jnp.sum(total[:, width:], axis=1, keepdims=True)
    row = lax.broadcasted_iota(jnp.int32, (ROWS, ROWS), 0)
    lane = lax.broadcasted_iota(jnp.int32, (ROWS, ROWS), 1)
    loss_ref[...] = jnp.sum(jnp.where(row == lane, loss, 0.0), axis=0)


def on_device(images, texts, scale, bias):
    width = images.shape[1]
    half, full = jnp.bfloat16, jnp.float32

    def shape(rows, columns, kind):
        return jax.ShapeDtypeStruct((rows, columns), kind)

    def exchange(value, axes, peers):
        pieces = value.reshape(peers, value.shape[0] // peers, value.shape[1])
        return lax.all_to_all(pieces, axes, 0, 0, tiled=True).reshape(value.shape)

    before = next_chip(texts, 1)
    spread = pl.pallas_call(
        spread_kernel,
        out_shape=shape(LINE * ROWS, width, half),
        in_specs=[VMEM],
        out_specs=VMEM,
        cost_estimate=pl.CostEstimate(flops=10**8, bytes_accessed=10**5, transcendentals=0),
        compiler_params=ROOM,
        name="spread",
    )(images)
    line_imgs = exchange(spread, "line", LINE)
    pairs = pl.pallas_call(
        pair_kernel,
        out_shape=shape(NEAR * 2 * ROWS, width, half),
        in_specs=[VMEM, VMEM],
        out_specs=VMEM,
        compiler_params=ROOM,
        cost_estimate=pl.CostEstimate(flops=2*10**10, bytes_accessed=10**6, transcendentals=0),
        name="pair",
    )(texts, before)
    pairs, line_imgs = lax.optimization_barrier((pairs, line_imgs))
    near_txts = exchange(pairs, ("core", "ring"), NEAR)
    gu_parts, gv_parts = pl.pallas_call(
        score_kernel,
        out_shape=(shape(LINE * ROWS, width + LANES, half), shape(NEAR * 2 * ROWS, width, half)),
        in_specs=[SMEM, SMEM, VMEM, VMEM],
        out_specs=(VMEM, VMEM),
        compiler_params=ROOM,
        name="score",
    )(scale.reshape(1), bias.reshape(1), line_imgs, near_txts)
    gv_parts = exchange(gv_parts, ("core", "ring"), NEAR)
    gu_parts = exchange(gu_parts, "line", LINE)
    own, back = pl.pallas_call(
        near_sum_kernel,
        out_shape=(shape(ROWS, width, full), shape(ROWS, width, half)),
        in_specs=[VMEM],
        out_specs=(VMEM, VMEM),
        compiler_params=ROOM,
        name="near_sum",
    )(gv_parts)
    back = next_chip(back, -1)
    return pl.pallas_call(
        finish_kernel,
        out_shape=(
            shape(ROWS, width, full),
            shape(ROWS, width, full),
            jax.ShapeDtypeStruct((ROWS,), full),
        ),
        in_specs=[VMEM] * 5,
        out_specs=(VMEM, VMEM, VMEM),
        compiler_params=ROOM,
        name="finish",
    )(gu_parts, images, texts, own, back)


def solution(mesh):
    parts = Mesh(mesh.devices.reshape(FAR, X, CORE, LINE, RING), AXES)
    rows = P(AXES, None)
    return jax.shard_map(
        on_device,
        mesh=parts,
        in_specs=(rows, rows, P(), P()),
        out_specs=(rows, rows, P(AXES)),
        check_vma=False,
    )
```

```python
import jax
import jax.numpy as jnp
from jax import lax
from jax.experimental import pallas as pl
from jax.experimental.pallas import tpu as pltpu
from jax.sharding import Mesh, PartitionSpec as P

EPS = 1e-06
ROUNDS = 3
ROWS = 8
AXES = ("far", "x", "core", "line", "ring")
FAR, X, CORE, LINE, RING = 4, 4, 2, 8, 4
CHIPS = ("far", "x")
NEAR = CORE * RING
LANES = 128
SMEM = pl.BlockSpec(memory_space=pltpu.SMEM)
VMEM = pl.BlockSpec(memory_space=pltpu.VMEM)
ROOM = pltpu.CompilerParams(vmem_limit_bytes=8 * 2**20)


def next_chip(value, steps):
    count = FAR * X
    return lax.ppermute(value, CHIPS, [(s, (s + steps) % count) for s in range(count)])


def normalize(x):
    xf = x.astype(jnp.float32)
    norms = jnp.sqrt(jnp.sum(xf * xf, axis=-1, keepdims=True) + EPS)
    return xf / norms, norms


def project_back(grad, unit, norms):
    return (grad - unit * jnp.sum(unit * grad, axis=-1, keepdims=True)) / norms


def spread_kernel(img_ref, out_ref):
    img = img_ref[...].astype(jnp.float32)
    out_ref[...] = jnp.concatenate([img] * LINE).astype(out_ref.dtype)


def pair_kernel(own_ref, before_ref, after_ref, out_ref):
    del after_ref
    pair = [own_ref[...].astype(jnp.float32), before_ref[...].astype(jnp.float32)]
    out_ref[...] = jnp.concatenate(pair * NEAR).astype(out_ref.dtype)


def score_kernel(scale_ref, bias_ref, img_ref, txt_ref, gu_ref, gv_ref):
    scale, bias = scale_ref[0], bias_ref[0]
    core, line, ring = lax.axis_index("core"), lax.axis_index("line"), lax.axis_index("ring")
    img = normalize(img_ref[...])[0].astype(jnp.bfloat16)
    txt = normalize(txt_ref[...])[0].astype(jnp.bfloat16)
    dots = lax.dot_general(img, txt, (((1,), (1,)), ((), ())), preferred_element_type=jnp.float32)
    logit = scale * dots + bias
    row = lax.broadcasted_iota(jnp.int32, logit.shape, 0)
    column = lax.broadcasted_iota(jnp.int32, logit.shape, 1)
    back = core - column // (RING * 2 * ROWS) + 2 * (column // ROWS % 2)
    scored = (back >= 0) & (back < ROUNDS)
    row = row - line * ROWS
    own = (row >= 0) & (row < ROWS) & (column == (core * RING + ring) * (2 * ROWS) + row)
    against = jnp.where(own, -logit, logit)
    decay = jnp.exp(-jnp.abs(against))
    loss = jnp.where(scored, jnp.maximum(against, 0.0) + jnp.log1p(decay), 0.0)
    chance = jnp.where(against >= 0, 1.0, decay) / (1.0 + decay)
    coef = jnp.where(scored, jnp.where(own, -chance, chance) * scale, 0.0)
    width = img.shape[1]
    gv_ref[...] = jnp.dot(
        coef.T.astype(jnp.bfloat16), img, preferred_element_type=jnp.float32
    ).astype(jnp.bfloat16)
    gu_ref[:, :width] = jnp.dot(
        coef.astype(jnp.bfloat16), txt, preferred_element_type=jnp.float32
    ).astype(jnp.bfloat16)
    total = jnp.sum(loss, axis=1, keepdims=True)
    high = total.astype(jnp.bfloat16).astype(jnp.float32)
    lane = lax.broadcasted_iota(jnp.int32, (total.shape[0], LANES), 1)
    gu_ref[:, width:] = jnp.where(
        lane == 0, high, jnp.where(lane == 1, total - high, 0.0)
    ).astype(jnp.bfloat16)


def near_sum_kernel(parts_ref, own_ref, back_ref):
    parts = parts_ref[...].astype(jnp.float32)
    total = jnp.sum(parts.reshape(NEAR, 2 * ROWS, parts.shape[1]), axis=0)
    own_ref[...] = total[:ROWS]
    back_ref[...] = total[ROWS:].astype(back_ref.dtype)


def finish_kernel(parts_ref, img_ref, txt_ref, own_ref, back_ref, ig_ref, tg_ref, loss_ref):
    width = img_ref.shape[1]
    parts = parts_ref[...].astype(jnp.float32)
    total = jnp.sum(parts.reshape(LINE, ROWS, parts.shape[1]), axis=0)
    ig_ref[...] = project_back(total[:, :width], *normalize(img_ref[...]))
    gv = own_ref[...] + back_ref[...].astype(jnp.float32)
    tg_ref[...] = project_back(gv, *normalize(txt_ref[...]))
    loss = jnp.sum(total[:, width:], axis=1, keepdims=True)
    row = lax.broadcasted_iota(jnp.int32, (ROWS, ROWS), 0)
    lane = lax.broadcasted_iota(jnp.int32, (ROWS, ROWS), 1)
    loss_ref[...] = jnp.sum(jnp.where(row == lane, loss, 0.0), axis=0)


def on_device(images, texts, scale, bias):
    width = images.shape[1]
    half, full = jnp.bfloat16, jnp.float32

    def shape(rows, columns, kind):
        return jax.ShapeDtypeStruct((rows, columns), kind)

    def exchange(value, axes, peers):
        pieces = value.reshape(peers, value.shape[0] // peers, value.shape[1])
        return lax.all_to_all(pieces, axes, 0, 0, tiled=True).reshape(value.shape)

    before = next_chip(texts, 1)
    spread = pl.pallas_call(
        spread_kernel,
        out_shape=shape(LINE * ROWS, width, half),
        in_specs=[VMEM],
        out_specs=VMEM,
        compiler_params=ROOM,
        name="spread",
    )(images)
    line_imgs = exchange(spread, "line", LINE)
    pairs = pl.pallas_call(
        pair_kernel,
        out_shape=shape(NEAR * 2 * ROWS, width, half),
        in_specs=[VMEM, VMEM, pl.BlockSpec(memory_space=pl.ANY)],
        out_specs=VMEM,
        compiler_params=ROOM,
        name="pair",
    )(texts, before, line_imgs)
    near_txts = exchange(pairs, ("core", "ring"), NEAR)
    gu_parts, gv_parts = pl.pallas_call(
        score_kernel,
        out_shape=(shape(LINE * ROWS, width + LANES, half), shape(NEAR * 2 * ROWS, width, half)),
        in_specs=[SMEM, SMEM, VMEM, VMEM],
        out_specs=(VMEM, VMEM),
        compiler_params=ROOM,
        name="score",
    )(scale.reshape(1), bias.reshape(1), line_imgs, near_txts)
    gv_parts = exchange(gv_parts, ("core", "ring"), NEAR)
    gu_parts = exchange(gu_parts, "line", LINE)
    own, back = pl.pallas_call(
        near_sum_kernel,
        out_shape=(shape(ROWS, width, full), shape(ROWS, width, half)),
        in_specs=[VMEM],
        out_specs=(VMEM, VMEM),
        compiler_params=ROOM,
        name="near_sum",
    )(gv_parts)
    back = next_chip(back, -1)
    return pl.pallas_call(
        finish_kernel,
        out_shape=(
            shape(ROWS, width, full),
            shape(ROWS, width, full),
            jax.ShapeDtypeStruct((ROWS,), full),
        ),
        in_specs=[VMEM] * 5,
        out_specs=(VMEM, VMEM, VMEM),
        compiler_params=ROOM,
        name="finish",
    )(gu_parts, images, texts, own, back)


def solution(mesh):
    parts = Mesh(mesh.devices.reshape(FAR, X, CORE, LINE, RING), AXES)
    rows = P(AXES, None)
    return jax.shard_map(
        on_device,
        mesh=parts,
        in_specs=(rows, rows, P(), P()),
        out_specs=(rows, rows, P(AXES)),
        check_vma=False,
    )
```

```python
import jax
import jax.numpy as jnp
from jax import lax
from jax.experimental import pallas as pl
from jax.experimental.pallas import tpu as pltpu
from jax.sharding import Mesh, PartitionSpec as P

EPS = 1e-06
ROUNDS = 3
ROWS = 8
AXES = ("far", "x", "core", "line", "ring")
FAR, X, CORE, LINE, RING = 4, 4, 2, 8, 4
CHIPS = ("far", "x")
NEAR = CORE * RING
LANES = 128
SMEM = pl.BlockSpec(memory_space=pltpu.SMEM)
VMEM = pl.BlockSpec(memory_space=pltpu.VMEM)
ROOM = pltpu.CompilerParams(vmem_limit_bytes=8 * 2**20)


def next_chip(value, steps):
    count = FAR * X
    return lax.ppermute(value, CHIPS, [(s, (s + steps) % count) for s in range(count)])


def normalize(x):
    xf = x.astype(jnp.float32)
    norms = jnp.sqrt(jnp.sum(xf * xf, axis=-1, keepdims=True) + EPS)
    return xf / norms, norms


def project_back(grad, unit, norms):
    return (grad - unit * jnp.sum(unit * grad, axis=-1, keepdims=True)) / norms


def spread_kernel(img_ref, out_ref):
    img = img_ref[...].astype(jnp.float32)
    out_ref[...] = jnp.concatenate([img] * LINE).astype(out_ref.dtype)


def pair_kernel(own_ref, before_ref, after_ref, out_ref):
    del after_ref
    pair = [own_ref[...].astype(jnp.float32), before_ref[...].astype(jnp.float32)]
    out_ref[...] = jnp.concatenate(pair * NEAR).astype(out_ref.dtype)


def score_kernel(scale_ref, bias_ref, img_ref, txt_ref, gu_ref, gv_ref):
    scale, bias = scale_ref[0], bias_ref[0]
    core, line, ring = lax.axis_index("core"), lax.axis_index("line"), lax.axis_index("ring")
    img = normalize(img_ref[...])[0].astype(jnp.bfloat16)
    txt = normalize(txt_ref[...])[0].astype(jnp.bfloat16)
    dots = lax.dot_general(img, txt, (((1,), (1,)), ((), ())), preferred_element_type=jnp.float32)
    logit = scale * dots + bias
    row = lax.broadcasted_iota(jnp.int32, logit.shape, 0)
    column = lax.broadcasted_iota(jnp.int32, logit.shape, 1)
    back = core - column // (RING * 2 * ROWS) + 2 * (column // ROWS % 2)
    scored = (back >= 0) & (back < ROUNDS)
    row = row - line * ROWS
    own = (row >= 0) & (row < ROWS) & (column == (core * RING + ring) * (2 * ROWS) + row)
    against = jnp.where(own, -logit, logit)
    decay = jnp.exp(-jnp.abs(against))
    loss = jnp.where(scored, jnp.maximum(against, 0.0) + jnp.log1p(decay), 0.0)
    chance = jnp.where(against >= 0, 1.0, decay) / (1.0 + decay)
    coef = jnp.where(scored, jnp.where(own, -chance, chance) * scale, 0.0)
    width = img.shape[1]
    gv_ref[...] = jnp.dot(
        coef.T.astype(jnp.bfloat16), img, preferred_element_type=jnp.float32
    ).astype(jnp.bfloat16)
    gu_ref[:, :width] = jnp.dot(
        coef.astype(jnp.bfloat16), txt, preferred_element_type=jnp.float32
    ).astype(jnp.bfloat16)
    total = jnp.sum(loss, axis=1, keepdims=True)
    high = total.astype(jnp.bfloat16).astype(jnp.float32)
    lane = lax.broadcasted_iota(jnp.int32, (total.shape[0], LANES), 1)
    gu_ref[:, width:] = jnp.where(
        lane == 0, high, jnp.where(lane == 1, total - high, 0.0)
    ).astype(jnp.bfloat16)


def near_sum_kernel(parts_ref, own_ref, back_ref):
    parts = parts_ref[...].astype(jnp.float32)
    total = jnp.sum(parts.reshape(NEAR, 2 * ROWS, parts.shape[1]), axis=0)
    own_ref[...] = total[:ROWS]
    back_ref[...] = total[ROWS:].astype(back_ref.dtype)


def finish_texts_kernel(txt_ref, own_ref, back_ref, tg_ref):
    gv = own_ref[...] + back_ref[...].astype(jnp.float32)
    tg_ref[...] = project_back(gv, *normalize(txt_ref[...]))


def finish_images_kernel(parts_ref, img_ref, ig_ref, loss_ref):
    width = img_ref.shape[1]
    parts = parts_ref[...].astype(jnp.float32)
    total = jnp.sum(parts.reshape(LINE, ROWS, parts.shape[1]), axis=0)
    ig_ref[...] = project_back(total[:, :width], *normalize(img_ref[...]))
    loss = jnp.sum(total[:, width:], axis=1, keepdims=True)
    row = lax.broadcasted_iota(jnp.int32, (ROWS, ROWS), 0)
    lane = lax.broadcasted_iota(jnp.int32, (ROWS, ROWS), 1)
    loss_ref[...] = jnp.sum(jnp.where(row == lane, loss, 0.0), axis=0)


def on_device(images, texts, scale, bias):
    width = images.shape[1]
    half, full = jnp.bfloat16, jnp.float32

    def shape(rows, columns, kind):
        return jax.ShapeDtypeStruct((rows, columns), kind)

    def exchange(value, axes, peers):
        pieces = value.reshape(peers, value.shape[0] // peers, value.shape[1])
        return lax.all_to_all(pieces, axes, 0, 0, tiled=True).reshape(value.shape)

    before = next_chip(texts, 1)
    spread = pl.pallas_call(
        spread_kernel,
        out_shape=shape(LINE * ROWS, width, half),
        in_specs=[VMEM],
        out_specs=VMEM,
        compiler_params=ROOM,
        name="spread",
    )(images)
    line_imgs = exchange(spread, "line", LINE)
    pairs = pl.pallas_call(
        pair_kernel,
        out_shape=shape(NEAR * 2 * ROWS, width, half),
        in_specs=[VMEM, VMEM, pl.BlockSpec(memory_space=pl.ANY)],
        out_specs=VMEM,
        compiler_params=ROOM,
        name="pair",
    )(texts, before, line_imgs)
    near_txts = exchange(pairs, ("core", "ring"), NEAR)
    gu_parts, gv_parts = pl.pallas_call(
        score_kernel,
        out_shape=(shape(LINE * ROWS, width + LANES, half), shape(NEAR * 2 * ROWS, width, half)),
        in_specs=[SMEM, SMEM, VMEM, VMEM],
        out_specs=(VMEM, VMEM),
        compiler_params=ROOM,
        name="score",
    )(scale.reshape(1), bias.reshape(1), line_imgs, near_txts)
    gv_parts = exchange(gv_parts, ("core", "ring"), NEAR)
    own, back = pl.pallas_call(
        near_sum_kernel,
        out_shape=(shape(ROWS, width, full), shape(ROWS, width, half)),
        in_specs=[VMEM],
        out_specs=(VMEM, VMEM),
        compiler_params=ROOM,
        name="near_sum",
    )(gv_parts)
    gu_parts, own, back = lax.optimization_barrier((gu_parts, own, back))
    back = next_chip(back, -1)
    gu_parts = exchange(gu_parts, "line", LINE)
    text_grad = pl.pallas_call(
        finish_texts_kernel,
        out_shape=shape(ROWS, width, full),
        in_specs=[VMEM] * 3,
        out_specs=VMEM,
        compiler_params=ROOM,
        cost_estimate=pl.CostEstimate(flops=2 * 10**10, bytes_accessed=10**6, transcendentals=0),
        name="finish_texts",
    )(texts, own, back)
    image_grad, loss = pl.pallas_call(
        finish_images_kernel,
        out_shape=(shape(ROWS, width, full), jax.ShapeDtypeStruct((ROWS,), full)),
        in_specs=[VMEM] * 2,
        out_specs=(VMEM, VMEM),
        compiler_params=ROOM,
        name="finish_images",
    )(gu_parts, images)
    return image_grad, text_grad, loss


def solution(mesh):
    parts = Mesh(mesh.devices.reshape(FAR, X, CORE, LINE, RING), AXES)
    rows = P(AXES, None)
    return jax.shard_map(
        on_device,
        mesh=parts,
        in_specs=(rows, rows, P(), P()),
        out_specs=(rows, rows, P(AXES)),
        check_vma=False,
    )
```

```python
import jax
import jax.numpy as jnp
from jax import lax
from jax.experimental import pallas as pl
from jax.experimental.pallas import tpu as pltpu
from jax.sharding import Mesh, PartitionSpec as P

EPS = 1e-06
ROUNDS = 3
ROWS = 8
AXES = ("far", "x", "core", "line", "ring")
FAR, X, CORE, LINE, RING = 4, 4, 2, 8, 4
CHIPS = ("far", "x")
SHARE = ROUNDS * ROWS
LANES = 128
SMEM = pl.BlockSpec(memory_space=pltpu.SMEM)
VMEM = pl.BlockSpec(memory_space=pltpu.VMEM)
ROOM = pltpu.CompilerParams(vmem_limit_bytes=8 * 2**20)


def next_chip(value, steps):
    count = FAR * X
    return lax.ppermute(value, CHIPS, [(s, (s + steps) % count) for s in range(count)])


def normalize(x):
    xf = x.astype(jnp.float32)
    norms = jnp.sqrt(jnp.sum(xf * xf, axis=-1, keepdims=True) + EPS)
    return xf / norms, norms


def project_back(grad, unit, norms):
    return (grad - unit * jnp.sum(unit * grad, axis=-1, keepdims=True)) / norms


def spread_kernel(img_ref, txt_ref, out_ref):
    width = img_ref.shape[1]
    for ref, columns in ((img_ref, slice(0, width)), (txt_ref, slice(width, 2 * width))):
        shard = ref[...].astype(jnp.float32)
        out_ref[:, columns] = jnp.concatenate([shard] * LINE).astype(out_ref.dtype)


def mate_kernel(img_ref, txt_ref, after_ref, before_ref, out_ref):
    first = lax.axis_index("core") == 0
    img, txt, after, before = (
        ref[...].astype(jnp.float32) for ref in (img_ref, txt_ref, after_ref, before_ref)
    )
    pair = [jnp.where(first, txt, before), jnp.where(first, after, img)]
    out_ref[...] = jnp.concatenate(pair).astype(out_ref.dtype)


def pack_kernel(img_ref, txt_ref, after_ref, before_ref, mate_ref, out_ref):
    img, txt, after, before, mate = (
        ref[...].astype(jnp.float32) for ref in (img_ref, txt_ref, after_ref, before_ref, mate_ref)
    )
    parts = [txt, mate[:ROWS], before, img, mate[ROWS:], after]
    out_ref[...] = jnp.concatenate(parts).astype(out_ref.dtype)


def score_kernel(scale_ref, bias_ref, line_ref, ring_ref, out_ref):
    scale, bias = scale_ref[0], bias_ref[0]
    line, ring = lax.axis_index("line"), lax.axis_index("ring")
    width = ring_ref.shape[1]
    around = normalize(ring_ref[...])[0].reshape(RING, 2, SHARE, width)

    def against(ours, others):
        ours = normalize(ours)[0].astype(jnp.bfloat16)
        others = others.reshape(RING * SHARE, width).astype(jnp.bfloat16)
        dots = lax.dot_general(
            ours, others, (((1,), (1,)), ((), ())), preferred_element_type=jnp.float32
        )
        logit = scale * dots + bias
        row = lax.broadcasted_iota(jnp.int32, logit.shape, 0) - line * ROWS
        column = lax.broadcasted_iota(jnp.int32, logit.shape, 1) - ring * SHARE
        own = (row == column) & (row >= 0) & (row < ROWS)
        signed = jnp.where(own, -logit, logit)
        decay = jnp.exp(-jnp.abs(signed))
        chance = jnp.where(signed >= 0, 1.0, decay) / (1.0 + decay)
        coef = jnp.where(own, -chance, chance) * scale
        grad = jnp.dot(coef.astype(jnp.bfloat16), others, preferred_element_type=jnp.float32)
        return grad.astype(jnp.bfloat16), signed, decay

    out_ref[:, width : 2 * width] = against(line_ref[:, width:], around[:, 1])[0]
    grad, signed, decay = against(line_ref[:, :width], around[:, 0])
    out_ref[:, :width] = grad
    loss = jnp.maximum(signed, 0.0) + jnp.log1p(decay)
    total = jnp.sum(loss, axis=1, keepdims=True)
    high = total.astype(jnp.bfloat16).astype(jnp.float32)
    lane = lax.broadcasted_iota(jnp.int32, (total.shape[0], LANES), 1)
    out_ref[:, 2 * width :] = jnp.where(
        lane == 0, high, jnp.where(lane == 1, total - high, 0.0)
    ).astype(jnp.bfloat16)


def finish_kernel(parts_ref, img_ref, txt_ref, ig_ref, tg_ref, loss_ref):
    width = img_ref.shape[1]
    parts = parts_ref[...].astype(jnp.float32)
    total = jnp.sum(parts.reshape(LINE, ROWS, parts.shape[1]), axis=0)
    ig_ref[...] = project_back(total[:, :width], *normalize(img_ref[...]))
    tg_ref[...] = project_back(total[:, width : 2 * width], *normalize(txt_ref[...]))
    loss = jnp.sum(total[:, 2 * width :], axis=1, keepdims=True)
    row = lax.broadcasted_iota(jnp.int32, (ROWS, ROWS), 0)
    lane = lax.broadcasted_iota(jnp.int32, (ROWS, ROWS), 1)
    loss_ref[...] = jnp.sum(jnp.where(row == lane, loss, 0.0), axis=0)


def on_device(images, texts, scale, bias):
    width = images.shape[1]
    half, full = jnp.bfloat16, jnp.float32

    def shape(rows, columns, kind):
        return jax.ShapeDtypeStruct((rows, columns), kind)

    def line_exchange(value):
        pieces = value.reshape(LINE, ROWS, value.shape[1])
        return lax.all_to_all(pieces, "line", 0, 0, tiled=True).reshape(value.shape)

    before = next_chip(texts, 1)
    after = next_chip(images, -1)
    spread = pl.pallas_call(
        spread_kernel,
        out_shape=shape(LINE * ROWS, 2 * width, half),
        in_specs=[VMEM] * 2,
        out_specs=VMEM,
        compiler_params=ROOM,
        name="spread",
    )(images, texts)
    line = line_exchange(spread)
    mate = pl.pallas_call(
        mate_kernel,
        out_shape=shape(2 * ROWS, width, half),
        in_specs=[VMEM] * 4,
        out_specs=VMEM,
        compiler_params=ROOM,
        cost_estimate=pl.CostEstimate(flops=2 * 10**10, bytes_accessed=10**6, transcendentals=0),
        name="mate",
    )(images, texts, after, before)
    mate = lax.ppermute(mate, "core", [(0, 1), (1, 0)])
    pack = pl.pallas_call(
        pack_kernel,
        out_shape=shape(2 * SHARE, width, half),
        in_specs=[VMEM] * 5,
        out_specs=VMEM,
        compiler_params=ROOM,
        name="pack",
    )(images, texts, after, before, mate)
    ring = lax.all_gather(pack, "ring", axis=0, tiled=True)
    parts = pl.pallas_call(
        score_kernel,
        out_shape=shape(LINE * ROWS, 2 * width + LANES, half),
        in_specs=[SMEM, SMEM, VMEM, VMEM],
        out_specs=VMEM,
        compiler_params=ROOM,
        name="score",
    )(scale.reshape(1), bias.reshape(1), line, ring)
    parts = line_exchange(parts)
    return pl.pallas_call(
        finish_kernel,
        out_shape=(
            shape(ROWS, width, full),
            shape(ROWS, width, full),
            jax.ShapeDtypeStruct((ROWS,), full),
        ),
        in_specs=[VMEM] * 3,
        out_specs=(VMEM, VMEM, VMEM),
        compiler_params=ROOM,
        name="finish",
    )(parts, images, texts)


def solution(mesh):
    parts = Mesh(mesh.devices.reshape(FAR, X, CORE, LINE, RING), AXES)
    rows = P(AXES, None)
    return jax.shard_map(
        on_device,
        mesh=parts,
        in_specs=(rows, rows, P(), P()),
        out_specs=(rows, rows, P(AXES)),
        check_vma=False,
    )
```

```python
import jax
import jax.numpy as jnp
from jax import lax
from jax.experimental import pallas as pl
from jax.experimental.pallas import tpu as pltpu
from jax.sharding import Mesh, PartitionSpec as P

EPS = 1e-06
ROUNDS = 3
ROWS = 8
AXES = ("far", "x", "core", "line", "ring")
FAR, X, CORE, LINE, RING = 4, 4, 2, 8, 4
CHIPS = ("far", "x")
SHARE = ROUNDS * ROWS
LANES = 128
SMEM = pl.BlockSpec(memory_space=pltpu.SMEM)
VMEM = pl.BlockSpec(memory_space=pltpu.VMEM)
ROOM = pltpu.CompilerParams(vmem_limit_bytes=8 * 2**20)


def with_neighbour(value, first):
    count = FAR * X
    pairs = [(chip, (chip + 1) % count) for chip in range(first, count, 2)]
    return lax.ppermute(value, CHIPS, pairs + [(b, a) for a, b in pairs])


def normalize(x):
    xf = x.astype(jnp.float32)
    norms = jnp.sqrt(jnp.sum(xf * xf, axis=-1, keepdims=True) + EPS)
    return xf / norms, norms


def project_back(grad, unit, norms):
    return (grad - unit * jnp.sum(unit * grad, axis=-1, keepdims=True)) / norms


def spread_kernel(img_ref, txt_ref, out_ref):
    width = img_ref.shape[1]
    for ref, columns in ((img_ref, slice(0, width)), (txt_ref, slice(width, 2 * width))):
        shard = ref[...].astype(jnp.float32)
        out_ref[:, columns] = jnp.concatenate([shard] * LINE).astype(out_ref.dtype)


def visitors(near, far):
    even = (lax.axis_index("x") & 1) == 0
    near, far = near.astype(jnp.float32), far.astype(jnp.float32)
    return jnp.where(even, near, far), jnp.where(even, far, near)


def mate_kernel(img_ref, txt_ref, near_ref, far_ref, out_ref):
    first = lax.axis_index("core") == 0
    img, txt = img_ref[...].astype(jnp.float32), txt_ref[...].astype(jnp.float32)
    after, before = visitors(near_ref[...], far_ref[...])
    pair = [jnp.where(first, txt, before), jnp.where(first, after, img)]
    out_ref[...] = jnp.concatenate(pair).astype(out_ref.dtype)


def pack_kernel(img_ref, txt_ref, near_ref, far_ref, mate_ref, out_ref):
    img, txt, mate = (ref[...].astype(jnp.float32) for ref in (img_ref, txt_ref, mate_ref))
    after, before = visitors(near_ref[...], far_ref[...])
    parts = [txt, mate[:ROWS], before, img, mate[ROWS:], after]
    out_ref[...] = jnp.concatenate(parts).astype(out_ref.dtype)


def score_kernel(scale_ref, bias_ref, line_ref, ring_ref, out_ref):
    scale, bias = scale_ref[0], bias_ref[0]
    line, ring = lax.axis_index("line"), lax.axis_index("ring")
    width = ring_ref.shape[1]
    around = normalize(ring_ref[...])[0].reshape(RING, 2, SHARE, width)

    def against(ours, others):
        ours = normalize(ours)[0].astype(jnp.bfloat16)
        others = others.reshape(RING * SHARE, width).astype(jnp.bfloat16)
        dots = lax.dot_general(
            ours, others, (((1,), (1,)), ((), ())), preferred_element_type=jnp.float32
        )
        logit = scale * dots + bias
        row = lax.broadcasted_iota(jnp.int32, logit.shape, 0) - line * ROWS
        column = lax.broadcasted_iota(jnp.int32, logit.shape, 1) - ring * SHARE
        own = (row == column) & (row >= 0) & (row < ROWS)
        signed = jnp.where(own, -logit, logit)
        decay = jnp.exp(-jnp.abs(signed))
        chance = jnp.where(signed >= 0, 1.0, decay) / (1.0 + decay)
        coef = jnp.where(own, -chance, chance) * scale
        grad = jnp.dot(coef.astype(jnp.bfloat16), others, preferred_element_type=jnp.float32)
        return grad.astype(jnp.bfloat16), signed, decay

    out_ref[:, width : 2 * width] = against(line_ref[:, width:], around[:, 1])[0]
    grad, signed, decay = against(line_ref[:, :width], around[:, 0])
    out_ref[:, :width] = grad
    loss = jnp.maximum(signed, 0.0) + jnp.log1p(decay)
    total = jnp.sum(loss, axis=1, keepdims=True)
    high = total.astype(jnp.bfloat16).astype(jnp.float32)
    lane = lax.broadcasted_iota(jnp.int32, (total.shape[0], LANES), 1)
    out_ref[:, 2 * width :] = jnp.where(
        lane == 0, high, jnp.where(lane == 1, total - high, 0.0)
    ).astype(jnp.bfloat16)


def finish_kernel(parts_ref, img_ref, txt_ref, ig_ref, tg_ref, loss_ref):
    width = img_ref.shape[1]
    parts = parts_ref[...].astype(jnp.float32)
    total = jnp.sum(parts.reshape(LINE, ROWS, parts.shape[1]), axis=0)
    ig_ref[...] = project_back(total[:, :width], *normalize(img_ref[...]))
    tg_ref[...] = project_back(total[:, width : 2 * width], *normalize(txt_ref[...]))
    loss = jnp.sum(total[:, 2 * width :], axis=1, keepdims=True)
    row = lax.broadcasted_iota(jnp.int32, (ROWS, ROWS), 0)
    lane = lax.broadcasted_iota(jnp.int32, (ROWS, ROWS), 1)
    loss_ref[...] = jnp.sum(jnp.where(row == lane, loss, 0.0), axis=0)


def on_device(images, texts, scale, bias):
    width = images.shape[1]
    half, full = jnp.bfloat16, jnp.float32

    def shape(rows, columns, kind):
        return jax.ShapeDtypeStruct((rows, columns), kind)

    def line_exchange(value):
        pieces = value.reshape(LINE, ROWS, value.shape[1])
        return lax.all_to_all(pieces, "line", 0, 0, tiled=True).reshape(value.shape)

    even = (lax.axis_index("x") & 1) == 0
    far = with_neighbour(jnp.where(even, images, texts), 1)
    near = with_neighbour(jnp.where(even, texts, images), 0)
    spread = pl.pallas_call(
        spread_kernel,
        out_shape=shape(LINE * ROWS, 2 * width, half),
        in_specs=[VMEM] * 2,
        out_specs=VMEM,
        name="spread",
    )(images, texts)
    line = line_exchange(spread)
    mate = pl.pallas_call(
        mate_kernel,
        out_shape=shape(2 * ROWS, width, half),
        in_specs=[VMEM] * 4,
        out_specs=VMEM,
        compiler_params=ROOM,
        cost_estimate=pl.CostEstimate(flops=2 * 10**10, bytes_accessed=10**6, transcendentals=0),
        name="mate",
    )(images, texts, near, far)
    mate = lax.ppermute(mate, "core", [(0, 1), (1, 0)])
    pack = pl.pallas_call(
        pack_kernel,
        out_shape=shape(2 * SHARE, width, half),
        in_specs=[VMEM] * 5,
        out_specs=VMEM,
        compiler_params=ROOM,
        name="pack",
    )(images, texts, near, far, mate)
    ring = lax.all_gather(pack, "ring", axis=0, tiled=True)
    parts = pl.pallas_call(
        score_kernel,
        out_shape=shape(LINE * ROWS, 2 * width + LANES, half),
        in_specs=[SMEM, SMEM, VMEM, VMEM],
        out_specs=VMEM,
        compiler_params=ROOM,
        name="score",
    )(scale.reshape(1), bias.reshape(1), line, ring)
    parts = line_exchange(parts)
    return pl.pallas_call(
        finish_kernel,
        out_shape=(
            shape(ROWS, width, full),
            shape(ROWS, width, full),
            jax.ShapeDtypeStruct((ROWS,), full),
        ),
        in_specs=[VMEM] * 3,
        out_specs=(VMEM, VMEM, VMEM),
        compiler_params=ROOM,
        name="finish",
    )(parts, images, texts)


def solution(mesh):
    parts = Mesh(mesh.devices.reshape(FAR, X, CORE, LINE, RING), AXES)
    rows = P(AXES, None)
    return jax.shard_map(
        on_device,
        mesh=parts,
        in_specs=(rows, rows, P(), P()),
        out_specs=(rows, rows, P(AXES)),
        check_vma=False,
    )
```

```python
import jax
import jax.numpy as jnp
from jax import lax
from jax.experimental import pallas as pl
from jax.experimental.pallas import tpu as pltpu
from jax.sharding import Mesh, PartitionSpec as P

EPS = 1e-06
ROUNDS = 3
ROWS = 8
AXES = ("far", "x", "core", "line", "ring")
FAR, X, CORE, LINE, RING = 4, 4, 2, 8, 4
CHIPS = ("far", "x")
SHARE = ROUNDS * ROWS
LANES = 128
SMEM = pl.BlockSpec(memory_space=pltpu.SMEM)
VMEM = pl.BlockSpec(memory_space=pltpu.VMEM)
ROOM = pltpu.CompilerParams(vmem_limit_bytes=8 * 2**20)


def with_neighbour(value, first):
    count = FAR * X
    pairs = [(chip, (chip + 1) % count) for chip in range(first, count, 2)]
    return lax.ppermute(value, CHIPS, pairs + [(b, a) for a, b in pairs])


def normalize(x):
    xf = x.astype(jnp.float32)
    norms = jnp.sqrt(jnp.sum(xf * xf, axis=-1, keepdims=True) + EPS)
    return xf / norms, norms


def project_back(grad, unit, norms):
    return (grad - unit * jnp.sum(unit * grad, axis=-1, keepdims=True)) / norms


def open_kernel(img_ref, txt_ref, near_ref, far_ref, line_ref):
    even = (lax.axis_index("x") & 1) == 0
    width = img_ref.shape[1]
    img, txt = img_ref[...].astype(jnp.float32), txt_ref[...].astype(jnp.float32)
    near_ref[...] = jnp.where(even, txt, img).astype(near_ref.dtype)
    far_ref[...] = jnp.where(even, img, txt).astype(far_ref.dtype)
    line_ref[:, :width] = jnp.concatenate([img] * LINE).astype(line_ref.dtype)
    line_ref[:, width:] = jnp.concatenate([txt] * LINE).astype(line_ref.dtype)


def visitors(near, far):
    even = (lax.axis_index("x") & 1) == 0
    near, far = near.astype(jnp.float32), far.astype(jnp.float32)
    return jnp.where(even, near, far), jnp.where(even, far, near)


def mate_kernel(img_ref, txt_ref, near_ref, far_ref, out_ref):
    first = lax.axis_index("core") == 0
    img, txt = img_ref[...].astype(jnp.float32), txt_ref[...].astype(jnp.float32)
    after, before = visitors(near_ref[...], far_ref[...])
    pair = [jnp.where(first, txt, before), jnp.where(first, after, img)]
    out_ref[...] = jnp.concatenate(pair).astype(out_ref.dtype)


def pack_kernel(img_ref, txt_ref, near_ref, far_ref, mate_ref, out_ref):
    img, txt, mate = (ref[...].astype(jnp.float32) for ref in (img_ref, txt_ref, mate_ref))
    after, before = visitors(near_ref[...], far_ref[...])
    parts = [txt, mate[:ROWS], before, img, mate[ROWS:], after]
    out_ref[...] = jnp.concatenate(parts).astype(out_ref.dtype)


def score_kernel(scale_ref, bias_ref, line_ref, ring_ref, out_ref):
    scale, bias = scale_ref[0], bias_ref[0]
    line, ring = lax.axis_index("line"), lax.axis_index("ring")
    width = ring_ref.shape[1]
    around = normalize(ring_ref[...])[0].reshape(RING, 2, SHARE, width)

    def against(ours, others):
        ours = normalize(ours)[0].astype(jnp.bfloat16)
        others = others.reshape(RING * SHARE, width).astype(jnp.bfloat16)
        dots = lax.dot_general(
            ours, others, (((1,), (1,)), ((), ())), preferred_element_type=jnp.float32
        )
        logit = scale * dots + bias
        row = lax.broadcasted_iota(jnp.int32, logit.shape, 0) - line * ROWS
        column = lax.broadcasted_iota(jnp.int32, logit.shape, 1) - ring * SHARE
        own = (row == column) & (row >= 0) & (row < ROWS)
        signed = jnp.where(own, -logit, logit)
        decay = jnp.exp(-jnp.abs(signed))
        chance = jnp.where(signed >= 0, 1.0, decay) / (1.0 + decay)
        coef = jnp.where(own, -chance, chance) * scale
        grad = jnp.dot(coef.astype(jnp.bfloat16), others, preferred_element_type=jnp.float32)
        return grad.astype(jnp.bfloat16), signed, decay

    out_ref[:, width : 2 * width] = against(line_ref[:, width:], around[:, 1])[0]
    grad, signed, decay = against(line_ref[:, :width], around[:, 0])
    out_ref[:, :width] = grad
    loss = jnp.maximum(signed, 0.0) + jnp.log1p(decay)
    total = jnp.sum(loss, axis=1, keepdims=True)
    high = total.astype(jnp.bfloat16).astype(jnp.float32)
    lane = lax.broadcasted_iota(jnp.int32, (total.shape[0], LANES), 1)
    out_ref[:, 2 * width :] = jnp.where(
        lane == 0, high, jnp.where(lane == 1, total - high, 0.0)
    ).astype(jnp.bfloat16)


def finish_kernel(parts_ref, img_ref, txt_ref, ig_ref, tg_ref, loss_ref):
    width = img_ref.shape[1]
    parts = parts_ref[...].astype(jnp.float32)
    total = jnp.sum(parts.reshape(LINE, ROWS, parts.shape[1]), axis=0)
    ig_ref[...] = project_back(total[:, :width], *normalize(img_ref[...]))
    tg_ref[...] = project_back(total[:, width : 2 * width], *normalize(txt_ref[...]))
    loss = jnp.sum(total[:, 2 * width :], axis=1, keepdims=True)
    row = lax.broadcasted_iota(jnp.int32, (ROWS, ROWS), 0)
    lane = lax.broadcasted_iota(jnp.int32, (ROWS, ROWS), 1)
    loss_ref[...] = jnp.sum(jnp.where(row == lane, loss, 0.0), axis=0)


def on_device(images, texts, scale, bias):
    width = images.shape[1]
    half, full = jnp.bfloat16, jnp.float32

    def shape(rows, columns, kind):
        return jax.ShapeDtypeStruct((rows, columns), kind)

    def line_exchange(value):
        pieces = value.reshape(LINE, ROWS, value.shape[1])
        return lax.all_to_all(pieces, "line", 0, 0, tiled=True).reshape(value.shape)

    near, far, spread = pl.pallas_call(
        open_kernel,
        out_shape=(
            shape(ROWS, width, half),
            shape(ROWS, width, half),
            shape(LINE * ROWS, 2 * width, half),
        ),
        in_specs=[VMEM] * 2,
        out_specs=(VMEM,) * 3,
        name="open",
    )(images, texts)
    far = with_neighbour(far, 1)
    near = with_neighbour(near, 0)
    line = line_exchange(spread)
    mate = pl.pallas_call(
        mate_kernel,
        out_shape=shape(2 * ROWS, width, half),
        in_specs=[VMEM] * 4,
        out_specs=VMEM,
        compiler_params=ROOM,
        cost_estimate=pl.CostEstimate(flops=2 * 10**10, bytes_accessed=10**6, transcendentals=0),
        name="mate",
    )(images, texts, near, far)
    mate = lax.ppermute(mate, "core", [(0, 1), (1, 0)])
    pack = pl.pallas_call(
        pack_kernel,
        out_shape=shape(2 * SHARE, width, half),
        in_specs=[VMEM] * 5,
        out_specs=VMEM,
        compiler_params=ROOM,
        name="pack",
    )(images, texts, near, far, mate)
    ring = lax.all_gather(pack, "ring", axis=0, tiled=True)
    parts = pl.pallas_call(
        score_kernel,
        out_shape=shape(LINE * ROWS, 2 * width + LANES, half),
        in_specs=[SMEM, SMEM, VMEM, VMEM],
        out_specs=VMEM,
        compiler_params=ROOM,
        name="score",
    )(scale.reshape(1), bias.reshape(1), line, ring)
    parts = line_exchange(parts)
    return pl.pallas_call(
        finish_kernel,
        out_shape=(
            shape(ROWS, width, full),
            shape(ROWS, width, full),
            jax.ShapeDtypeStruct((ROWS,), full),
        ),
        in_specs=[VMEM] * 3,
        out_specs=(VMEM, VMEM, VMEM),
        compiler_params=ROOM,
        name="finish",
    )(parts, images, texts)


def solution(mesh):
    parts = Mesh(mesh.devices.reshape(FAR, X, CORE, LINE, RING), AXES)
    rows = P(AXES, None)
    return jax.shard_map(
        on_device,
        mesh=parts,
        in_specs=(rows, rows, P(), P()),
        out_specs=(rows, rows, P(AXES)),
        check_vma=False,
    )
```

```python
import jax
import jax.numpy as jnp
from jax import lax
from jax.experimental import pallas as pl
from jax.experimental.pallas import tpu as pltpu
from jax.sharding import Mesh, PartitionSpec as P

EPS = 1e-06
ROUNDS = 3
ROWS = 8
AXES = ("far", "x", "core", "line", "ring")
FAR, X, CORE, LINE, RING = 4, 4, 2, 8, 4
CHIPS = ("far", "x")
SHARE = ROUNDS * ROWS
LANES = 128
ORDER = (4, 5, 6, 7, 0, 1, 2, 3)
SMEM = pl.BlockSpec(memory_space=pltpu.SMEM)
VMEM = pl.BlockSpec(memory_space=pltpu.VMEM)
ROOM = pltpu.CompilerParams(vmem_limit_bytes=8 * 2**20)


def with_neighbour(value, first):
    count = FAR * X
    pairs = [(chip, (chip + 1) % count) for chip in range(first, count, 2)]
    return lax.ppermute(value, CHIPS, pairs + [(b, a) for a, b in pairs])


def normalize(x):
    xf = x.astype(jnp.float32)
    norms = jnp.sqrt(jnp.sum(xf * xf, axis=-1, keepdims=True) + EPS)
    return xf / norms, norms


def project_back(grad, unit, norms):
    return (grad - unit * jnp.sum(unit * grad, axis=-1, keepdims=True)) / norms


def open_kernel(img_ref, txt_ref, near_ref, far_ref, line_ref):
    even = (lax.axis_index("x") & 1) == 0
    width = img_ref.shape[1]
    img, txt = img_ref[...].astype(jnp.float32), txt_ref[...].astype(jnp.float32)
    near_ref[...] = jnp.where(even, txt, img).astype(near_ref.dtype)
    far_ref[...] = jnp.where(even, img, txt).astype(far_ref.dtype)
    line_ref[:, :width] = jnp.concatenate([img] * LINE).astype(line_ref.dtype)
    line_ref[:, width:] = jnp.concatenate([txt] * LINE).astype(line_ref.dtype)


def visitors(near, far):
    even = (lax.axis_index("x") & 1) == 0
    near, far = near.astype(jnp.float32), far.astype(jnp.float32)
    return jnp.where(even, near, far), jnp.where(even, far, near)


def mate_kernel(img_ref, txt_ref, near_ref, far_ref, out_ref):
    first = lax.axis_index("core") == 0
    img, txt = img_ref[...].astype(jnp.float32), txt_ref[...].astype(jnp.float32)
    after, before = visitors(near_ref[...], far_ref[...])
    pair = [jnp.where(first, txt, before), jnp.where(first, after, img)]
    out_ref[...] = jnp.concatenate(pair).astype(out_ref.dtype)


def pack_kernel(img_ref, txt_ref, near_ref, far_ref, mate_ref, out_ref):
    img, txt, mate = (ref[...].astype(jnp.float32) for ref in (img_ref, txt_ref, mate_ref))
    after, before = visitors(near_ref[...], far_ref[...])
    parts = [txt, mate[:ROWS], before, img, mate[ROWS:], after]
    out_ref[...] = jnp.concatenate(parts).astype(out_ref.dtype)


def score_kernel(scale_ref, bias_ref, line_ref, ring_ref, out_ref):
    scale, bias = scale_ref[0], bias_ref[0]
    line, ring = lax.axis_index("line"), lax.axis_index("ring")
    place = sum(jnp.where(line == at, slot, 0) for slot, at in enumerate(ORDER))
    width = ring_ref.shape[1]
    around = normalize(ring_ref[...])[0].reshape(RING, 2, SHARE, width)

    def against(ours, others):
        ours = normalize(ours)[0].astype(jnp.bfloat16)
        others = others.reshape(RING * SHARE, width).astype(jnp.bfloat16)
        dots = lax.dot_general(
            ours, others, (((1,), (1,)), ((), ())), preferred_element_type=jnp.float32
        )
        logit = scale * dots + bias
        row = lax.broadcasted_iota(jnp.int32, logit.shape, 0) - place * ROWS
        column = lax.broadcasted_iota(jnp.int32, logit.shape, 1) - ring * SHARE
        own = (row == column) & (row >= 0) & (row < ROWS)
        signed = jnp.where(own, -logit, logit)
        decay = jnp.exp(-jnp.abs(signed))
        chance = jnp.where(signed >= 0, 1.0, decay) / (1.0 + decay)
        coef = jnp.where(own, -chance, chance) * scale
        grad = jnp.dot(coef.astype(jnp.bfloat16), others, preferred_element_type=jnp.float32)
        return grad.astype(jnp.bfloat16), signed, decay

    out_ref[:, width : 2 * width] = against(line_ref[:, width:], around[:, 1])[0]
    grad, signed, decay = against(line_ref[:, :width], around[:, 0])
    out_ref[:, :width] = grad
    loss = jnp.maximum(signed, 0.0) + jnp.log1p(decay)
    total = jnp.sum(loss, axis=1, keepdims=True)
    high = total.astype(jnp.bfloat16).astype(jnp.float32)
    lane = lax.broadcasted_iota(jnp.int32, (total.shape[0], LANES), 1)
    out_ref[:, 2 * width :] = jnp.where(
        lane == 0, high, jnp.where(lane == 1, total - high, 0.0)
    ).astype(jnp.bfloat16)


def finish_kernel(parts_ref, img_ref, txt_ref, ig_ref, tg_ref, loss_ref):
    width = img_ref.shape[1]
    parts = parts_ref[...].astype(jnp.float32)
    total = jnp.sum(parts.reshape(LINE, ROWS, parts.shape[1]), axis=0)
    ig_ref[...] = project_back(total[:, :width], *normalize(img_ref[...]))
    tg_ref[...] = project_back(total[:, width : 2 * width], *normalize(txt_ref[...]))
    loss = jnp.sum(total[:, 2 * width :], axis=1, keepdims=True)
    row = lax.broadcasted_iota(jnp.int32, (ROWS, ROWS), 0)
    lane = lax.broadcasted_iota(jnp.int32, (ROWS, ROWS), 1)
    loss_ref[...] = jnp.sum(jnp.where(row == lane, loss, 0.0), axis=0)


def on_device(images, texts, scale, bias):
    width = images.shape[1]
    half, full = jnp.bfloat16, jnp.float32

    def shape(rows, columns, kind):
        return jax.ShapeDtypeStruct((rows, columns), kind)

    def line_exchange(value):
        pieces = value.reshape(LINE, ROWS, value.shape[1])
        return lax.all_to_all(
            pieces, "line", 0, 0, tiled=True, axis_index_groups=[list(ORDER)]
        ).reshape(value.shape)

    near, far, spread = pl.pallas_call(
        open_kernel,
        out_shape=(
            shape(ROWS, width, half),
            shape(ROWS, width, half),
            shape(LINE * ROWS, 2 * width, half),
        ),
        in_specs=[VMEM] * 2,
        out_specs=(VMEM,) * 3,
        name="open",
    )(images, texts)
    far = with_neighbour(far, 1)
    near = with_neighbour(near, 0)
    line = line_exchange(spread)
    mate = pl.pallas_call(
        mate_kernel,
        out_shape=shape(2 * ROWS, width, half),
        in_specs=[VMEM] * 4,
        out_specs=VMEM,
        compiler_params=ROOM,
        cost_estimate=pl.CostEstimate(flops=2 * 10**10, bytes_accessed=10**6, transcendentals=0),
        name="mate",
    )(images, texts, near, far)
    mate = lax.ppermute(mate, "core", [(0, 1), (1, 0)])
    pack = pl.pallas_call(
        pack_kernel,
        out_shape=shape(2 * SHARE, width, half),
        in_specs=[VMEM] * 5,
        out_specs=VMEM,
        compiler_params=ROOM,
        name="pack",
    )(images, texts, near, far, mate)
    ring = lax.all_gather(pack, "ring", axis=0, tiled=True)
    parts = pl.pallas_call(
        score_kernel,
        out_shape=shape(LINE * ROWS, 2 * width + LANES, half),
        in_specs=[SMEM, SMEM, VMEM, VMEM],
        out_specs=VMEM,
        compiler_params=ROOM,
        name="score",
    )(scale.reshape(1), bias.reshape(1), line, ring)
    parts = line_exchange(parts)
    return pl.pallas_call(
        finish_kernel,
        out_shape=(
            shape(ROWS, width, full),
            shape(ROWS, width, full),
            jax.ShapeDtypeStruct((ROWS,), full),
        ),
        in_specs=[VMEM] * 3,
        out_specs=(VMEM, VMEM, VMEM),
        compiler_params=ROOM,
        name="finish",
    )(parts, images, texts)


def solution(mesh):
    parts = Mesh(mesh.devices.reshape(FAR, X, CORE, LINE, RING), AXES)
    rows = P(AXES, None)
    return jax.shard_map(
        on_device,
        mesh=parts,
        in_specs=(rows, rows, P(), P()),
        out_specs=(rows, rows, P(AXES)),
        check_vma=False,
    )
```

```python
import jax
import jax.numpy as jnp
from jax import lax
from jax.experimental import pallas as pl
from jax.experimental.pallas import tpu as pltpu
from jax.sharding import Mesh, PartitionSpec as P

EPS = 1e-06
ROUNDS = 3
ROWS = 8
AXES = ("far", "x", "core", "line", "ring")
FAR, X, CORE, LINE, RING = 4, 4, 2, 8, 4
CHIPS = ("far", "x")
SHARE = ROUNDS * ROWS
LANES = 128
OUT = (3, 4, 5, 6, 7, 0, 1, 2)
BACK = (4, 5, 6, 7, 0, 1, 2, 3)
SMEM = pl.BlockSpec(memory_space=pltpu.SMEM)
VMEM = pl.BlockSpec(memory_space=pltpu.VMEM)
ROOM = pltpu.CompilerParams(vmem_limit_bytes=8 * 2**20)


def with_neighbour(value, first):
    count = FAR * X
    pairs = [(chip, (chip + 1) % count) for chip in range(first, count, 2)]
    return lax.ppermute(value, CHIPS, pairs + [(b, a) for a, b in pairs])


def normalize(x):
    xf = x.astype(jnp.float32)
    norms = jnp.sqrt(jnp.sum(xf * xf, axis=-1, keepdims=True) + EPS)
    return xf / norms, norms


def project_back(grad, unit, norms):
    return (grad - unit * jnp.sum(unit * grad, axis=-1, keepdims=True)) / norms


def open_kernel(img_ref, txt_ref, near_ref, far_ref, line_ref):
    even = (lax.axis_index("x") & 1) == 0
    width = img_ref.shape[1]
    img, txt = img_ref[...].astype(jnp.float32), txt_ref[...].astype(jnp.float32)
    near_ref[...] = jnp.where(even, txt, img).astype(near_ref.dtype)
    far_ref[...] = jnp.where(even, img, txt).astype(far_ref.dtype)
    line_ref[:, :width] = jnp.concatenate([img] * LINE).astype(line_ref.dtype)
    line_ref[:, width:] = jnp.concatenate([txt] * LINE).astype(line_ref.dtype)


def visitors(near, far):
    even = (lax.axis_index("x") & 1) == 0
    near, far = near.astype(jnp.float32), far.astype(jnp.float32)
    return jnp.where(even, near, far), jnp.where(even, far, near)


def mate_kernel(img_ref, txt_ref, near_ref, far_ref, out_ref):
    first = lax.axis_index("core") == 0
    img, txt = img_ref[...].astype(jnp.float32), txt_ref[...].astype(jnp.float32)
    after, before = visitors(near_ref[...], far_ref[...])
    pair = [jnp.where(first, txt, before), jnp.where(first, after, img)]
    out_ref[...] = jnp.concatenate(pair).astype(out_ref.dtype)


def pack_kernel(img_ref, txt_ref, near_ref, far_ref, mate_ref, out_ref):
    img, txt, mate = (ref[...].astype(jnp.float32) for ref in (img_ref, txt_ref, mate_ref))
    after, before = visitors(near_ref[...], far_ref[...])
    parts = [txt, mate[:ROWS], before, img, mate[ROWS:], after]
    out_ref[...] = jnp.concatenate(parts).astype(out_ref.dtype)


def score_kernel(scale_ref, bias_ref, line_ref, ring_ref, out_ref):
    scale, bias = scale_ref[0], bias_ref[0]
    line, ring = lax.axis_index("line"), lax.axis_index("ring")
    place = sum(jnp.where(line == at, slot, 0) for slot, at in enumerate(BACK))
    width = ring_ref.shape[1]
    around = normalize(ring_ref[...])[0].reshape(RING, 2, SHARE, width)

    def against(ours, others):
        ours = normalize(ours)[0].reshape(LINE, ROWS, width)
        ours = jnp.concatenate([ours[OUT.index(at)] for at in BACK]).astype(jnp.bfloat16)
        others = others.reshape(RING * SHARE, width).astype(jnp.bfloat16)
        dots = lax.dot_general(
            ours, others, (((1,), (1,)), ((), ())), preferred_element_type=jnp.float32
        )
        logit = scale * dots + bias
        row = lax.broadcasted_iota(jnp.int32, logit.shape, 0) - place * ROWS
        column = lax.broadcasted_iota(jnp.int32, logit.shape, 1) - ring * SHARE
        own = (row == column) & (row >= 0) & (row < ROWS)
        signed = jnp.where(own, -logit, logit)
        decay = jnp.exp(-jnp.abs(signed))
        chance = jnp.where(signed >= 0, 1.0, decay) / (1.0 + decay)
        coef = jnp.where(own, -chance, chance) * scale
        grad = jnp.dot(coef.astype(jnp.bfloat16), others, preferred_element_type=jnp.float32)
        return grad.astype(jnp.bfloat16), signed, decay

    out_ref[:, width : 2 * width] = against(line_ref[:, width:], around[:, 1])[0]
    grad, signed, decay = against(line_ref[:, :width], around[:, 0])
    out_ref[:, :width] = grad
    loss = jnp.maximum(signed, 0.0) + jnp.log1p(decay)
    total = jnp.sum(loss, axis=1, keepdims=True)
    high = total.astype(jnp.bfloat16).astype(jnp.float32)
    lane = lax.broadcasted_iota(jnp.int32, (total.shape[0], LANES), 1)
    out_ref[:, 2 * width :] = jnp.where(
        lane == 0, high, jnp.where(lane == 1, total - high, 0.0)
    ).astype(jnp.bfloat16)


def finish_kernel(parts_ref, img_ref, txt_ref, ig_ref, tg_ref, loss_ref):
    width = img_ref.shape[1]
    parts = parts_ref[...].astype(jnp.float32)
    total = jnp.sum(parts.reshape(LINE, ROWS, parts.shape[1]), axis=0)
    ig_ref[...] = project_back(total[:, :width], *normalize(img_ref[...]))
    tg_ref[...] = project_back(total[:, width : 2 * width], *normalize(txt_ref[...]))
    loss = jnp.sum(total[:, 2 * width :], axis=1, keepdims=True)
    row = lax.broadcasted_iota(jnp.int32, (ROWS, ROWS), 0)
    lane = lax.broadcasted_iota(jnp.int32, (ROWS, ROWS), 1)
    loss_ref[...] = jnp.sum(jnp.where(row == lane, loss, 0.0), axis=0)


def on_device(images, texts, scale, bias):
    width = images.shape[1]
    half, full = jnp.bfloat16, jnp.float32

    def shape(rows, columns, kind):
        return jax.ShapeDtypeStruct((rows, columns), kind)

    def line_exchange(value, order):
        pieces = value.reshape(LINE, ROWS, value.shape[1])
        return lax.all_to_all(
            pieces, "line", 0, 0, tiled=True, axis_index_groups=[list(order)]
        ).reshape(value.shape)

    near, far, spread = pl.pallas_call(
        open_kernel,
        out_shape=(
            shape(ROWS, width, half),
            shape(ROWS, width, half),
            shape(LINE * ROWS, 2 * width, half),
        ),
        in_specs=[VMEM] * 2,
        out_specs=(VMEM,) * 3,
        name="open",
    )(images, texts)
    far = with_neighbour(far, 1)
    near = with_neighbour(near, 0)
    line = line_exchange(spread, OUT)
    mate = pl.pallas_call(
        mate_kernel,
        out_shape=shape(2 * ROWS, width, half),
        in_specs=[VMEM] * 4,
        out_specs=VMEM,
        compiler_params=ROOM,
        cost_estimate=pl.CostEstimate(flops=2 * 10**10, bytes_accessed=10**6, transcendentals=0),
        name="mate",
    )(images, texts, near, far)
    mate = lax.ppermute(mate, "core", [(0, 1), (1, 0)])
    pack = pl.pallas_call(
        pack_kernel,
        out_shape=shape(2 * SHARE, width, half),
        in_specs=[VMEM] * 5,
        out_specs=VMEM,
        compiler_params=ROOM,
        name="pack",
    )(images, texts, near, far, mate)
    ring = lax.all_gather(pack, "ring", axis=0, tiled=True)
    parts = pl.pallas_call(
        score_kernel,
        out_shape=shape(LINE * ROWS, 2 * width + LANES, half),
        in_specs=[SMEM, SMEM, VMEM, VMEM],
        out_specs=VMEM,
        compiler_params=ROOM,
        name="score",
    )(scale.reshape(1), bias.reshape(1), line, ring)
    parts = line_exchange(parts, BACK)
    return pl.pallas_call(
        finish_kernel,
        out_shape=(
            shape(ROWS, width, full),
            shape(ROWS, width, full),
            jax.ShapeDtypeStruct((ROWS,), full),
        ),
        in_specs=[VMEM] * 3,
        out_specs=(VMEM, VMEM, VMEM),
        compiler_params=ROOM,
        name="finish",
    )(parts, images, texts)


def solution(mesh):
    parts = Mesh(mesh.devices.reshape(FAR, X, CORE, LINE, RING), AXES)
    rows = P(AXES, None)
    return jax.shard_map(
        on_device,
        mesh=parts,
        in_specs=(rows, rows, P(), P()),
        out_specs=(rows, rows, P(AXES)),
        check_vma=False,
    )
```

```python
import jax
import jax.numpy as jnp
from jax import lax
from jax.experimental import pallas as pl
from jax.experimental.pallas import tpu as pltpu
from jax.sharding import Mesh, PartitionSpec as P

EPS = 1e-06
ROUNDS = 3
ROWS = 8
AXES = ("far", "x", "core", "line", "ring")
FAR, X, CORE, LINE, RING = 4, 4, 2, 8, 4
CHIPS = ("far", "x")
SHARE = ROUNDS * ROWS
LANES = 128
OUT = (2, 3, 4, 5, 6, 7, 0, 1)
BACK = (4, 5, 6, 7, 0, 1, 2, 3)
SMEM = pl.BlockSpec(memory_space=pltpu.SMEM)
VMEM = pl.BlockSpec(memory_space=pltpu.VMEM)
ROOM = pltpu.CompilerParams(vmem_limit_bytes=8 * 2**20)


def with_neighbour(value, first):
    count = FAR * X
    pairs = [(chip, (chip + 1) % count) for chip in range(first, count, 2)]
    return lax.ppermute(value, CHIPS, pairs + [(b, a) for a, b in pairs])


def normalize(x):
    xf = x.astype(jnp.float32)
    norms = jnp.sqrt(jnp.sum(xf * xf, axis=-1, keepdims=True) + EPS)
    return xf / norms, norms


def project_back(grad, unit, norms):
    return (grad - unit * jnp.sum(unit * grad, axis=-1, keepdims=True)) / norms


def open_kernel(img_ref, txt_ref, near_ref, far_ref, line_ref):
    even = (lax.axis_index("x") & 1) == 0
    width = img_ref.shape[1]
    img, txt = img_ref[...].astype(jnp.float32), txt_ref[...].astype(jnp.float32)
    near_ref[...] = jnp.where(even, txt, img).astype(near_ref.dtype)
    far_ref[...] = jnp.where(even, img, txt).astype(far_ref.dtype)
    line_ref[:, :width] = jnp.concatenate([img] * LINE).astype(line_ref.dtype)
    line_ref[:, width:] = jnp.concatenate([txt] * LINE).astype(line_ref.dtype)


def visitors(near, far):
    even = (lax.axis_index("x") & 1) == 0
    near, far = near.astype(jnp.float32), far.astype(jnp.float32)
    return jnp.where(even, near, far), jnp.where(even, far, near)


def mate_kernel(img_ref, txt_ref, near_ref, far_ref, out_ref):
    first = lax.axis_index("core") == 0
    img, txt = img_ref[...].astype(jnp.float32), txt_ref[...].astype(jnp.float32)
    after, before = visitors(near_ref[...], far_ref[...])
    pair = [jnp.where(first, txt, before), jnp.where(first, after, img)]
    out_ref[...] = jnp.concatenate(pair).astype(out_ref.dtype)


def pack_kernel(img_ref, txt_ref, near_ref, far_ref, mate_ref, out_ref):
    img, txt, mate = (ref[...].astype(jnp.float32) for ref in (img_ref, txt_ref, mate_ref))
    after, before = visitors(near_ref[...], far_ref[...])
    parts = [txt, mate[:ROWS], before, img, mate[ROWS:], after]
    out_ref[...] = jnp.concatenate(parts).astype(out_ref.dtype)


def score_kernel(scale_ref, bias_ref, line_ref, ring_ref, out_ref):
    scale, bias = scale_ref[0], bias_ref[0]
    line, ring = lax.axis_index("line"), lax.axis_index("ring")
    place = sum(jnp.where(line == at, slot, 0) for slot, at in enumerate(BACK))
    width = ring_ref.shape[1]
    around = normalize(ring_ref[...])[0].reshape(RING, 2, SHARE, width)

    def against(ours, others):
        ours = normalize(ours)[0].reshape(LINE, ROWS, width)
        ours = jnp.concatenate([ours[OUT.index(at)] for at in BACK]).astype(jnp.bfloat16)
        others = others.reshape(RING * SHARE, width).astype(jnp.bfloat16)
        dots = lax.dot_general(
            ours, others, (((1,), (1,)), ((), ())), preferred_element_type=jnp.float32
        )
        logit = scale * dots + bias
        row = lax.broadcasted_iota(jnp.int32, logit.shape, 0) - place * ROWS
        column = lax.broadcasted_iota(jnp.int32, logit.shape, 1) - ring * SHARE
        own = (row == column) & (row >= 0) & (row < ROWS)
        signed = jnp.where(own, -logit, logit)
        decay = jnp.exp(-jnp.abs(signed))
        chance = jnp.where(signed >= 0, 1.0, decay) / (1.0 + decay)
        coef = jnp.where(own, -chance, chance) * scale
        grad = jnp.dot(coef.astype(jnp.bfloat16), others, preferred_element_type=jnp.float32)
        return grad.astype(jnp.bfloat16), signed, decay

    out_ref[:, width : 2 * width] = against(line_ref[:, width:], around[:, 1])[0]
    grad, signed, decay = against(line_ref[:, :width], around[:, 0])
    out_ref[:, :width] = grad
    loss = jnp.maximum(signed, 0.0) + jnp.log1p(decay)
    total = jnp.sum(loss, axis=1, keepdims=True)
    high = total.astype(jnp.bfloat16).astype(jnp.float32)
    lane = lax.broadcasted_iota(jnp.int32, (total.shape[0], LANES), 1)
    out_ref[:, 2 * width :] = jnp.where(
        lane == 0, high, jnp.where(lane == 1, total - high, 0.0)
    ).astype(jnp.bfloat16)


def finish_kernel(parts_ref, img_ref, txt_ref, ig_ref, tg_ref, loss_ref):
    width = img_ref.shape[1]
    parts = parts_ref[...].astype(jnp.float32)
    total = jnp.sum(parts.reshape(LINE, ROWS, parts.shape[1]), axis=0)
    ig_ref[...] = project_back(total[:, :width], *normalize(img_ref[...]))
    tg_ref[...] = project_back(total[:, width : 2 * width], *normalize(txt_ref[...]))
    loss = jnp.sum(total[:, 2 * width :], axis=1, keepdims=True)
    row = lax.broadcasted_iota(jnp.int32, (ROWS, ROWS), 0)
    lane = lax.broadcasted_iota(jnp.int32, (ROWS, ROWS), 1)
    loss_ref[...] = jnp.sum(jnp.where(row == lane, loss, 0.0), axis=0)


def on_device(images, texts, scale, bias):
    width = images.shape[1]
    half, full = jnp.bfloat16, jnp.float32

    def shape(rows, columns, kind):
        return jax.ShapeDtypeStruct((rows, columns), kind)

    def line_exchange(value, order):
        pieces = value.reshape(LINE, ROWS, value.shape[1])
        return lax.all_to_all(
            pieces, "line", 0, 0, tiled=True, axis_index_groups=[list(order)]
        ).reshape(value.shape)

    near, far, spread = pl.pallas_call(
        open_kernel,
        out_shape=(
            shape(ROWS, width, half),
            shape(ROWS, width, half),
            shape(LINE * ROWS, 2 * width, half),
        ),
        in_specs=[VMEM] * 2,
        out_specs=(VMEM,) * 3,
        name="open",
    )(images, texts)
    far = with_neighbour(far, 1)
    near = with_neighbour(near, 0)
    line = line_exchange(spread, OUT)
    mate = pl.pallas_call(
        mate_kernel,
        out_shape=shape(2 * ROWS, width, half),
        in_specs=[VMEM] * 4,
        out_specs=VMEM,
        compiler_params=ROOM,
        cost_estimate=pl.CostEstimate(flops=2 * 10**10, bytes_accessed=10**6, transcendentals=0),
        name="mate",
    )(images, texts, near, far)
    mate = lax.ppermute(mate, "core", [(0, 1), (1, 0)])
    pack = pl.pallas_call(
        pack_kernel,
        out_shape=shape(2 * SHARE, width, half),
        in_specs=[VMEM] * 5,
        out_specs=VMEM,
        compiler_params=ROOM,
        name="pack",
    )(images, texts, near, far, mate)
    ring = lax.all_gather(pack, "ring", axis=0, tiled=True)
    parts = pl.pallas_call(
        score_kernel,
        out_shape=shape(LINE * ROWS, 2 * width + LANES, half),
        in_specs=[SMEM, SMEM, VMEM, VMEM],
        out_specs=VMEM,
        compiler_params=ROOM,
        name="score",
    )(scale.reshape(1), bias.reshape(1), line, ring)
    parts = line_exchange(parts, BACK)
    return pl.pallas_call(
        finish_kernel,
        out_shape=(
            shape(ROWS, width, full),
            shape(ROWS, width, full),
            jax.ShapeDtypeStruct((ROWS,), full),
        ),
        in_specs=[VMEM] * 3,
        out_specs=(VMEM, VMEM, VMEM),
        compiler_params=ROOM,
        name="finish",
    )(parts, images, texts)


def solution(mesh):
    parts = Mesh(mesh.devices.reshape(FAR, X, CORE, LINE, RING), AXES)
    rows = P(AXES, None)
    return jax.shard_map(
        on_device,
        mesh=parts,
        in_specs=(rows, rows, P(), P()),
        out_specs=(rows, rows, P(AXES)),
        check_vma=False,
    )
```
